32 devices in a mesh: shard: 4 (over z), dp: 8 (over y, x, core).
Axes of the slice: x: 2, y: 2, z: 4, core: 2. Of those that a mesh axis runs over, the one named last changes fastest.
Arguments:
- cache_state: float32 [8, 4, 64, 384], P('dp', 'shard'), as said below
- table_state: float32 [8, 4, 128, 384], P('dp', 'shard'), as said below
- batch_idx: int32 [8, 4, 1024, 8], P('dp', 'shard'), may hold values from 0 to 63
- loss_grad: float32 [8, 4, 1024], P('dp', 'shard'), may hold values from -6 to 6
- w_first: bfloat16 [1024, 1024], replicated, may hold values from -0.1875 to 0.1875
- head: float32 [1024], replicated, may hold values from -6 to 6
- home: int32 [8, 512], P('dp'), may hold values from 0 to 511, as said below
- fetch_rows: int32 [8, 4, 4, 16], P('dp', 'shard'), may hold values from 0 to 511, as said below
- fetch_counts: int32 [8, 4, 4], P('dp', 'shard'), may hold values from 0 to 16, as said below
- evict_rows: int32 [8, 4, 4, 16], P('dp', 'shard'), may hold values from 0 to 511, as said below
- evict_from: int32 [8, 4, 4, 16], P('dp', 'shard'), may hold values from 0 to 63, as said below
- evict_counts: int32 [8, 4, 4], P('dp', 'shard'), may hold values from 0 to 16, as said below
Outputs:
- grad_first: bfloat16 [1024, 1024], P('shard')
- table_after: float32 [8, 4, 128, 384], P('dp', 'shard')
- fetched: float32 [8, 4, 4, 16, 384], P('dp', 'shard')
The draws below stay inside these ranges and needn't reach their ends.
Inputs may be any that keep to these rules, and one draw needn't show every extreme that they name: In each group home is a permutation; row r belongs to owner home[r] // 128. `fetch_rows`: every entry, live or not, names a row of the owner whose list it is in; no row is live both in a fetch list and in a write-back list of the same group. `fetch_counts`: in every group some owner gets 16 from every device. `evict_rows`: every entry names a row of the owner whose list it is in; live entries of a group are all different rows. `evict_from`: the entries of one device are all different. `evict_counts`: in every group some owner gets 16 from every device. `cache_state`: the last 128 entries of a row are positive. `table_state`: the last 128 entries of a row are positive.
All inputs are finite; a program needn't handle non-finite values.
Results may differ from the reference program's by a relative error of at most 0.0061.
Values sent between devices are 32-bit elements; how exact they have to be, the bound alone decides.
A program may use at most 64 MiB of HBM per device.

```python
import math
import jax
import jax.numpy as jnp
import numpy as np
from jax import lax

EMBED_DIM = 128
MLP_WIDTH = 1024
FEATURES = 8
TOK_DEV = 1024
CAPACITY = 16
CACHE_ROWS = 64
TABLE_ROWS = 128
GROUP_ROWS = 512
N_SHARD = 4
N_DP = 8


def state_block(key, rows):
    key_value, key_first, key_second = jax.random.split(key, 3)
    shape = (N_DP, N_SHARD, rows, EMBED_DIM)
    value = jax.random.normal(key_value, shape, jnp.float32)
    first = 0.1 * jax.random.normal(key_first, shape, jnp.float32)
    second = jnp.exp(jax.random.uniform(key_second, shape, jnp.float32, math.log(0.001), math.log(0.1)))
    return jnp.concatenate([value, first, second], axis=3)


def draw_cache_state(key, part):
    return state_block(jax.random.fold_in(key, 3), CACHE_ROWS)


def draw_table_state(key, part):
    return state_block(jax.random.fold_in(key, 5), TABLE_ROWS)


def busy_counts(key):
    key_base, key_busy = jax.random.split(key)
    base = jax.random.randint(key_base, (N_SHARD, N_SHARD), 0, CAPACITY + 1)
    busy = jax.random.randint(key_busy, (), 0, N_SHARD)
    column = jnp.arange(N_SHARD, dtype=jnp.int32)[None, :]
    return jnp.where(column == busy, CAPACITY, base).astype(jnp.int32)


def group_plan(key):
    key_home, key_order, key_evict, key_fetch, key_from = jax.random.split(key, 5)
    home = jax.random.permutation(key_home, GROUP_ROWS).astype(jnp.int32)
    inverse = jnp.argsort(home).astype(jnp.int32)
    orders = jax.vmap(lambda k: jax.random.permutation(k, TABLE_ROWS))(jax.random.split(key_order, N_SHARD)).astype(jnp.int32)
    owner = jnp.arange(N_SHARD, dtype=jnp.int32)[None, :, None]
    asker = jnp.arange(N_SHARD, dtype=jnp.int32)[:, None, None]
    within = jnp.arange(CAPACITY, dtype=jnp.int32)[None, None, :]
    position = asker * CAPACITY + within
    evict_slot = orders[owner, position]
    fetch_slot = orders[owner, N_SHARD * CAPACITY + position]
    evict_rows = inverse[owner * TABLE_ROWS + evict_slot].astype(jnp.int32)
    fetch_rows = inverse[owner * TABLE_ROWS + fetch_slot].astype(jnp.int32)
    sources = jax.vmap(lambda k: jax.random.permutation(k, CACHE_ROWS))(jax.random.split(key_from, N_SHARD))
    evict_from = sources.reshape(N_SHARD, N_SHARD, CAPACITY).astype(jnp.int32)
    return (home, fetch_rows, busy_counts(key_fetch), evict_rows, evict_from, busy_counts(key_evict))


def index_plan(key):
    keys = jax.random.split(jax.random.fold_in(key, 11), N_DP)
    return jax.vmap(group_plan)(keys)


def draw_home(key, part):
    return index_plan(key)[0]


def draw_fetch_rows(key, part):
    return index_plan(key)[1]


def draw_fetch_counts(key, part):
    return index_plan(key)[2]


def draw_evict_rows(key, part):
    return index_plan(key)[3]


def draw_evict_from(key, part):
    return index_plan(key)[4]


def draw_evict_counts(key, part):
    return index_plan(key)[5]


def plant(drawn, own_key, least, largest):
    dims = drawn.shape
    index_at = [jax.random.randint(jax.random.fold_in(own_key, axis), (), 0, dims[axis]) for axis in range(len(dims))]
    drawn = drawn.at[tuple(index_at)].set(least)
    longest = dims.index(max(dims))
    index_at[longest] = (index_at[longest] + 1) % dims[longest]
    return drawn.at[tuple(index_at)].set(largest)


def levels(own_key, extent, cuts, least, largest):
    gain, own = 1.0, jax.random.fold_in(own_key, 6)
    for axis_at, parts in cuts:
        steps = jnp.exp(jax.random.uniform(jax.random.fold_in(own, axis_at), (parts,), jnp.float32, least / len(cuts), largest / len(cuts)))
        gain = gain * jnp.repeat(steps, extent[axis_at] // parts).reshape([-1 if axis == axis_at else 1 for axis in range(len(extent))])
    return gain


def rank_bounds(number_of, slope):
    loads = [(1 << 20) // math.isqrt(rank ** slope) + 1 for rank in range(1, number_of + 1)]
    spread = 1 + sum(loads) // (1 << 30)
    return np.cumsum(np.array([max(1, weight // spread) for weight in loads]))


def skewed_ids(key, shape, count, slope):
    listing = rank_bounds(count, slope)
    pick = jax.random.randint(jax.random.fold_in(key, 1), shape, 0, int(listing[count - 1]))
    standing = jnp.searchsorted(jnp.asarray(listing, jnp.int32), pick, side="right")
    return jax.random.permutation(jax.random.fold_in(key, 2), count)[standing].astype(jnp.int32)


def noise(key, shape, scale, limit, shards=(), kind=jnp.bfloat16):
    factor_of = levels(key, shape, shards, -0.22, 0.18) if shards else 1.0
    values = jax.random.normal(key, shape, jnp.float32) * scale * factor_of
    return jnp.minimum(jnp.maximum(values, -limit), limit).astype(kind)


def setup_inputs(seed: int = 0) -> dict:
    arg_keys = jax.random.split(jax.random.key(seed), 13)
    return {
        "cache_state": draw_cache_state(jax.random.fold_in(arg_keys[12], 71), 0),
        "table_state": draw_table_state(jax.random.fold_in(arg_keys[12], 71), 0),
        "batch_idx": plant(skewed_ids(arg_keys[2], (N_DP, N_SHARD, TOK_DEV, FEATURES), CACHE_ROWS, 2), jax.random.fold_in(arg_keys[2], 3), 0, CACHE_ROWS - 1).astype(jnp.int32),
        "loss_grad": noise(arg_keys[3], (N_DP, N_SHARD, TOK_DEV), 1.0, 6.0, ((0, 8), (1, 4)), jnp.float32),
        "w_first": noise(arg_keys[4], (MLP_WIDTH, MLP_WIDTH), MLP_WIDTH ** -0.5, 0.1875),
        "head": noise(arg_keys[5], (MLP_WIDTH,), 1.0, 6.0, (), jnp.float32),
        "home": draw_home(jax.random.fold_in(arg_keys[12], 71), 0),
        "fetch_rows": draw_fetch_rows(jax.random.fold_in(arg_keys[12], 71), 0),
        "fetch_counts": draw_fetch_counts(jax.random.fold_in(arg_keys[12], 71), 0),
        "evict_rows": draw_evict_rows(jax.random.fold_in(arg_keys[12], 71), 0),
        "evict_from": draw_evict_from(jax.random.fold_in(arg_keys[12], 71), 0),
        "evict_counts": draw_evict_counts(jax.random.fold_in(arg_keys[12], 71), 0),
    }


beta_one = 0.9
beta_two = 0.999
learn_rate = 0.05
epsilon = 1e-08
bias_one = 1.0 - 0.9 ** 10
bias_two = 1.0 - 0.999 ** 10

def adam_rows(state, grads):
    value = state[:, :EMBED_DIM]
    first = state[:, EMBED_DIM:2 * EMBED_DIM]
    second = state[:, 2 * EMBED_DIM:]
    first = beta_one * first + (1.0 - beta_one) * grads
    second = beta_two * second + (1.0 - beta_two) * grads * grads
    value = value - learn_rate * (first / bias_one) / (jnp.sqrt(second / bias_two) + epsilon)
    return jnp.concatenate([value, first, second], axis=1)

def local_pass(cache, batch, loss, w_first, head):
    looked = jnp.take(cache[:, :EMBED_DIM], batch.reshape(-1), axis=0)
    inputs = looked.reshape(batch.shape[0], MLP_WIDTH).astype(jnp.bfloat16)
    pre = jnp.dot(inputs, w_first, preferred_element_type=jnp.float32)
    sigma = jax.nn.sigmoid(pre)
    delta = (loss[:, None] * head[None, :] * sigma * (1.0 + pre * (1.0 - sigma))).astype(jnp.bfloat16)
    term = lax.dot_general(inputs, delta, (((0,), (0,)), ((), ())), preferred_element_type=jnp.float32)
    back = lax.dot_general(delta, w_first, (((1,), (1,)), ((), ())), preferred_element_type=jnp.float32)
    grads = jax.ops.segment_sum(back.reshape(-1, EMBED_DIM), batch.reshape(-1), num_segments=cache.shape[0])
    return (term, adam_rows(cache, grads))

def settle(table_g, updated_g, home_g, ev_rows, ev_from, ev_counts, fe_rows, fe_counts):
    width = 3 * EMBED_DIM
    flat_table = table_g.reshape(GROUP_ROWS, width)
    within = jnp.arange(CAPACITY, dtype=jnp.int32)
    ev_live = within[None, None, :] < ev_counts[:, :, None]
    dest = jnp.where(ev_live, jnp.take(home_g, ev_rows, axis=0), GROUP_ROWS).astype(jnp.int32)
    source = jax.vmap(lambda rows, place: jnp.take(rows, place.reshape(-1), axis=0))(updated_g, ev_from)
    new_table = flat_table.at[dest.reshape(-1)].set(source.reshape(-1, width), mode='drop')
    fe_live = within[None, None, :] < fe_counts[:, :, None]
    place = jnp.take(home_g, fe_rows, axis=0).reshape(-1)
    got = jnp.take(flat_table, place, axis=0).reshape(N_SHARD, N_SHARD, CAPACITY, width)
    got = jnp.where(fe_live[..., None], got, jnp.zeros_like(got))
    return (new_table.reshape(N_SHARD, TABLE_ROWS, width), got)

def reference(cache_state, table_state, batch_idx, loss_grad, w_first, head, home, fetch_rows, fetch_counts, evict_rows, evict_from, evict_counts):
    count_all = N_DP * N_SHARD
    flat_cache = cache_state.reshape(count_all, CACHE_ROWS, 3 * EMBED_DIM)
    flat_batch = batch_idx.reshape(count_all, TOK_DEV, FEATURES)
    flat_loss = loss_grad.reshape(count_all, TOK_DEV)

    def step(total, item):
        term, updated = local_pass(item[0], item[1], item[2], w_first, head)
        return (total + term, updated)
    total, updated = lax.scan(step, jnp.zeros((MLP_WIDTH, MLP_WIDTH), jnp.float32), (flat_cache, flat_batch, flat_loss))
    grad_first = (total / math.sqrt(TOK_DEV * count_all)).astype(jnp.bfloat16)
    updated = updated.reshape(N_DP, N_SHARD, CACHE_ROWS, 3 * EMBED_DIM)
    table_after, fetched = jax.vmap(settle)(table_state, updated, home, evict_rows, evict_from, evict_counts, fetch_rows, fetch_counts)
    return (grad_first, table_after, fetched)
```

```python
import functools
import math

import jax
import jax.numpy as jnp
from jax import lax
from jax.experimental import pallas as pl
from jax.experimental.pallas import tpu as pltpu
from jax.sharding import PartitionSpec as P

beta_one = 0.9
beta_two = 0.999
learn_rate = 0.05
epsilon = 1e-08
bias_one = 1.0 - 0.9**10
bias_two = 1.0 - 0.999**10


def adam_rows(state, grads, embed):
    value = state[:, :embed]
    first = state[:, embed : 2 * embed]
    second = state[:, 2 * embed :]
    first = beta_one * first + (1.0 - beta_one) * grads
    second = beta_two * second + (1.0 - beta_two) * grads * grads
    value = value - learn_rate * (first / bias_one) / (jnp.sqrt(second / bias_two) + epsilon)
    return jnp.concatenate([value, first, second], axis=1)


def local(
    cache_state,
    table_state,
    batch_idx,
    loss_grad,
    w_first,
    head,
    home,
    fetch_rows,
    fetch_counts,
    evict_rows,
    evict_from,
    evict_counts,
):
    group = lax.axis_size("shard")
    cache = cache_state[0, 0]
    table = table_state[0, 0]
    batch = batch_idx[0, 0]
    loss = loss_grad[0, 0]
    home_map = home[0]
    wanted = fetch_rows[0, 0]
    gone = evict_rows[0, 0]
    gone_from = evict_from[0, 0]
    width = cache.shape[1]
    embed = width // 3
    table_rows = table.shape[0]
    cache_rows = cache.shape[0]
    capacity = wanted.shape[1]
    mlp_width = w_first.shape[0]
    samples = batch.shape[0]
    within = jnp.arange(capacity, dtype=jnp.int32)[None, :]
    wanted_live = within < fetch_counts[0, 0][:, None]
    gone_live = within < evict_counts[0, 0][:, None]
    place = (
        jnp.take(
            home_map,
            lax.all_to_all(wanted, "shard", split_axis=0, concat_axis=0, tiled=True),
            axis=0,
        )
        % table_rows
    )
    arrived = lax.all_to_all(
        jnp.take(table, place, axis=0), "shard", split_axis=0, concat_axis=0, tiled=True
    )
    flat_batch = batch.reshape(-1)
    looked = jnp.take(cache[:, :embed], flat_batch, axis=0)
    inputs = looked.reshape(samples, mlp_width).astype(jnp.bfloat16)
    pre = jnp.dot(inputs, w_first, preferred_element_type=jnp.float32)
    sigma = jax.nn.sigmoid(pre)
    delta = (loss[:, None] * head[None, :] * sigma * (1.0 + pre * (1.0 - sigma))).astype(
        jnp.bfloat16
    )
    back = lax.dot_general(
        delta, w_first, (((1,), (1,)), ((), ())), preferred_element_type=jnp.float32
    )
    positions = jnp.arange(cache_rows, dtype=jnp.int32)
    onehot = (flat_batch[:, None] == positions[None, :]).astype(jnp.float32)
    grads = lax.dot_general(
        onehot,
        back.reshape(-1, embed),
        (((0,), (0,)), ((), ())),
        precision=lax.Precision.HIGHEST,
        preferred_element_type=jnp.float32,
    )
    updated = adam_rows(cache, grads, embed)
    sent_rows = jnp.take(updated, gone_from.reshape(-1), axis=0).reshape(group, capacity, width)
    sent_slots = jnp.where(gone_live, jnp.take(home_map, gone, axis=0) % table_rows, table_rows)
    got_rows, got_slots = (
        lax.all_to_all(sent_rows, "shard", split_axis=0, concat_axis=0, tiled=True),
        lax.all_to_all(sent_slots, "shard", split_axis=0, concat_axis=0, tiled=True),
    )
    new_table = table.at[got_slots.reshape(-1)].set(got_rows.reshape(-1, width), mode="drop")
    fetched = jnp.where(wanted_live[:, :, None], arrived, jnp.zeros_like(arrived))
    scale = 1.0 / math.sqrt(samples * group * lax.axis_size("dp"))
    partial_rows = lax.psum_scatter(
        lax.dot_general(
            inputs, delta, (((0,), (0,)), ((), ())), preferred_element_type=jnp.float32
        ),
        "shard",
        scatter_dimension=0,
        tiled=True,
    )
    mine = lax.psum(partial_rows, "dp")
    grad_first = (mine * scale).astype(jnp.bfloat16)
    return (grad_first, new_table[None, None], fetched[None, None])


CHUNK = 256
PIECE = 16
BF = jnp.bfloat16
F32 = jnp.float32
EXACT = lax.Precision.HIGHEST


def dot(a, b, dims, precision=None):
    return lax.dot_general(
        a, b, (dims, ((), ())), precision=precision, preferred_element_type=F32
    )


NN = ((1,), (0,))
NT = ((1,), (1,))
TN = ((0,), (0,))


def split_two(a):
    high = a.astype(BF)
    return high, (a - high.astype(F32)).astype(BF)


def step_kernel(
    cache_ref,
    table_ref,
    batch_ref,
    loss_ref,
    w_ref,
    head_ref,
    home_ref,
    lists_ref,
    fetch_counts,
    evict_counts,
    grad_out,
    table_out,
    fetched_out,
    hot,
    hot_t,
    loss_col,
    base,
    delta,
    term,
    from_core,
    from_first,
    from_second,
    to_z,
    from_z,
    whole,
    slots_out,
    slots_in,
    rows_out,
    evict_out,
    evict_in,
    sum_send,
    sum_recv,
    row_send,
    row_recv,
):
    group = 4
    z = lax.axis_index("shard")
    dp = lax.axis_index("dp")
    core = dp % 2
    x = (dp // 2) % 2
    y = dp // 4
    by_core = {"dp": dp + 1 - 2 * core}
    by_x = {"dp": dp + 2 - 4 * x}
    by_y = {"dp": dp + 4 - 8 * y}
    near = (by_core, by_x, by_y)
    along = [{"shard": (z + d) % group} for d in range(1, group)]

    barrier = pltpu.get_barrier_semaphore()
    for device in near + tuple(along):
        pl.semaphore_signal(
            barrier, inc=1, device_id=device, device_id_type=pl.DeviceIdType.MESH
        )

    samples, features = batch_ref.shape[2], batch_ref.shape[3]
    cached = cache_ref.shape[2]
    embed = cache_ref.shape[3] // 3
    slots = table_ref.shape[2]
    width = w_ref.shape[1]
    capacity = fetched_out.shape[3]
    n_chunks = width // CHUNK
    columns = features * cached

    pending = []

    def send(src, dst, sends, recvs, at, device):
        copy = pltpu.make_async_remote_copy(
            src_ref=src,
            dst_ref=dst,
            send_sem=sends.at[at],
            recv_sem=recvs.at[at],
            device_id=device,
            device_id_type=pl.DeviceIdType.MESH,
        )
        copy.start()
        pending.append(copy)
        return copy

    home = (home_ref[...] % slots).astype(BF)
    home = jnp.broadcast_to(home.astype(F32), (8, home.shape[1])).astype(BF)
    listed = lists_ref[...]
    names = listed[:, : 2 * capacity]
    row_id = lax.broadcasted_iota(jnp.int32, (home.shape[1], 2 * capacity), 0)
    lane = lax.broadcasted_iota(jnp.int32, (8, 2 * capacity), 1)
    for j in range(group):
        hit = (row_id == names[j : j + 1, :]).astype(F32).astype(BF)
        found = dot(home, hit, NN).astype(jnp.int32)
        limit = jnp.where(lane < capacity, fetch_counts[0, 0, j], evict_counts[0, 0, j])
        found = jnp.where(lane % capacity < limit, found, -1)
        slots_out[j] = jnp.full(slots_out.shape[1:], -1, jnp.int32)
        slots_out[j, :, : 2 * capacity] = found
    slots_in[z] = slots_out[z]

    batch = batch_ref[0, 0].astype(F32).astype(BF)
    at_f = lax.broadcasted_iota(jnp.int32, (features, columns), 0)
    at_c = lax.broadcasted_iota(jnp.int32, (features, columns), 1)
    spread = (at_c // cached == at_f).astype(F32).astype(BF)
    at_f_t = lax.broadcasted_iota(jnp.int32, (columns, features), 1)
    at_c_t = lax.broadcasted_iota(jnp.int32, (columns, features), 0)
    spread_t = (at_c_t // cached == at_f_t).astype(F32).astype(BF)
    own_c = (lax.broadcasted_iota(jnp.int32, (samples, columns), 1) % cached).astype(F32)
    hot[...] = (dot(batch, spread, NN) == own_c).astype(F32).astype(BF)
    own_c_t = (lax.broadcasted_iota(jnp.int32, (columns, samples), 0) % cached).astype(F32)
    hot_t[...] = (dot(spread_t, batch, NT) == own_c_t).astype(F32).astype(BF)
    for t in range(samples // 128):
        piece = loss_ref[0, :, t * 128 : (t + 1) * 128]
        loss_col[t * 128 : (t + 1) * 128, :] = jnp.broadcast_to(piece, (128, 128)).T

    value = cache_ref[0, 0, :, :embed]
    value_bf = value.astype(BF)
    value_t = value.T.astype(BF)
    value_t2 = jnp.concatenate([value_t, value_t], axis=1)

    pl.semaphore_wait(barrier, len(near) + group - 1)
    slot_copies = []
    for d in range(1, group):
        peer = (z + d) % group
        slot_copies.append(
            send(slots_out.at[peer], slots_in.at[z], row_send, row_recv, d - 1, along[d - 1])
        )

    grads = [jnp.zeros((cached, embed), F32)]
    copies = {}
    n_sem = 13

    def compute(k):
        cols = slice(k * CHUNK, (k + 1) * CHUNK)
        for f in range(features):
            part = dot(value_bf, w_ref[f * embed : (f + 1) * embed, cols], NN)
            high, low = split_two(part)
            base[0, f * cached : (f + 1) * cached, :] = high
            base[1, f * cached : (f + 1) * cached, :] = low
        head = head_ref[:, cols]
        block = 256

        def rows(t, carry):
            at = pl.ds(pl.multiple_of(t * block, block), block)
            pre = dot(hot[at, :], base[0], NN) + dot(hot[at, :], base[1], NN)
            sigma = 1.0 / (1.0 + jnp.exp(-pre))
            loss = loss_col[at, :]
            loss = jnp.concatenate([loss] * (CHUNK // 128), axis=1)
            delta[at, :] = (loss * head * sigma * (1.0 + pre * (1.0 - sigma))).astype(BF)
            return carry

        lax.fori_loop(0, samples // block, rows, 0)
        for f in range(features):
            summed = dot(hot_t[f * cached : (f + 1) * cached, :], delta[...], NN)
            high, low = split_two(summed)
            both = jnp.concatenate([high, low], axis=0)
            piece = dot(value_t2, both, NN)
            term[k, f % 2, :, :, :, f // 2] = piece.reshape(2, 2, 2, PIECE, CHUNK)
            g = dot(both, w_ref[f * embed : (f + 1) * embed, cols], NT)
            grads[0] = grads[0] + g[:cached] + g[cached:]
        copies[k, 0] = send(
            term.at[k, 1 - core], from_core.at[k], sum_send, sum_recv, k * n_sem, by_core
        )

    def first(k):
        copies[k, 0].wait_recv()
        term[k, core] = term[k, core] + from_core[k]
        copies[k, 1] = send(
            term.at[k, core, 0, 1 - x], from_first.at[k, 0], sum_send, sum_recv, k * n_sem + 1, by_x
        )
        copies[k, 2] = send(
            term.at[k, core, 1, 1 - y], from_first.at[k, 1], sum_send, sum_recv, k * n_sem + 2, by_y
        )

    def second(k):
        copies[k, 1].wait_recv()
        term[k, core, 0, x] = term[k, core, 0, x] + from_first[k, 0]
        copies[k, 3] = send(
            term.at[k, core, 0, x, 1 - y], from_second.at[k, 0], sum_send, sum_recv, k * n_sem + 3, by_y
        )
        copies[k, 2].wait_recv()
        term[k, core, 1, y] = term[k, core, 1, y] + from_first[k, 1]
        copies[k, 4] = send(
            term.at[k, core, 1, y, 1 - x], from_second.at[k, 1], sum_send, sum_recv, k * n_sem + 4, by_x
        )

    def third(k):
        copies[k, 3].wait_recv()
        to_z[k, :, 0] = term[k, core, 0, x, y] + from_second[k, 0]
        copies[k, 4].wait_recv()
        to_z[k, :, 1] = term[k, core, 1, y, x] + from_second[k, 1]
        for d in range(1, group):
            peer = (z + d) % group
            copies[k, 4 + d] = send(
                to_z.at[k, peer], from_z.at[k, d - 1], sum_send, sum_recv, k * n_sem + 4 + d, along[d - 1]
            )

    def fourth(k):
        for d in range(1, group):
            copies[k, 4 + d].wait_recv()
        total = (to_z[k, z] + from_z[k, 0]) + (from_z[k, 1] + from_z[k, 2])
        whole[k, core, 0, x, y] = total[0]
        whole[k, core, 1, y, x] = total[1]
        mine = whole.at[k, core, 0, x, y]
        copies[k, 8] = send(mine, mine, sum_send, sum_recv, k * n_sem + 8, by_y)
        mine = whole.at[k, core, 1, y, x]
        copies[k, 9] = send(mine, mine, sum_send, sum_recv, k * n_sem + 9, by_x)

    def fifth(k):
        copies[k, 8].wait_recv()
        mine = whole.at[k, core, 0, x]
        copies[k, 10] = send(mine, mine, sum_send, sum_recv, k * n_sem + 10, by_x)
        copies[k, 9].wait_recv()
        mine = whole.at[k, core, 1, y]
        copies[k, 11] = send(mine, mine, sum_send, sum_recv, k * n_sem + 11, by_y)

    def sixth(k):
        copies[k, 10].wait_recv()
        copies[k, 11].wait_recv()
        mine = whole.at[k, core]
        copies[k, 12] = send(mine, mine, sum_send, sum_recv, k * n_sem + 12, by_core)

    scale = 1.0 / math.sqrt(samples * 32)

    def seventh(k):
        copies[k, 12].wait_recv()
        got = whole[k].reshape(16 * PIECE, CHUNK)
        grad_out[:, k * CHUNK : (k + 1) * CHUNK] = (got * scale).astype(BF)

    fetch_copies = []
    slot_id = lax.broadcasted_iota(jnp.int32, (slots, 2 * capacity), 0)
    slot_lane = lax.broadcasted_iota(jnp.int32, (slots, 2 * capacity), 1)

    def give():
        for copy in slot_copies:
            copy.wait_recv()
        for i in range(group):
            hit = (slot_id == slots_in[i, :1, : 2 * capacity]).astype(F32)
            rows = dot(hit, table_ref[0, 0], TN, EXACT)
            rows_out[i] = rows[:capacity]
        fetched_out[0, 0, z] = rows_out[z]
        for d in range(1, group):
            peer = (z + d) % group
            fetch_copies.append(
                send(rows_out.at[peer], fetched_out.at[0, 0, z], row_send, row_recv, 2 + d, along[d - 1])
            )

    evict_copies = []

    def write_back():
        state = cache_ref[0, 0]
        g = grads[0]
        moment = beta_one * state[:, embed : 2 * embed] + (1.0 - beta_one) * g
        second_moment = beta_two * state[:, 2 * embed :] + (1.0 - beta_two) * g * g
        new = state[:, :embed] - learn_rate * (moment / bias_one) / (
            jnp.sqrt(second_moment / bias_two) + epsilon
        )
        updated = jnp.concatenate([new, moment, second_moment], axis=1)
        position = lax.broadcasted_iota(jnp.int32, (cached, 3 * capacity), 0)
        for j in range(group):
            hit = (position == listed[j : j + 1, :]).astype(F32)
            rows = dot(hit, updated, TN, EXACT)
            evict_out[j] = rows[2 * capacity :]
        evict_in[z] = evict_out[z]
        for d in range(1, group):
            peer = (z + d) % group
            evict_copies.append(
                send(evict_out.at[peer], evict_in.at[z], row_send, row_recv, 5 + d, along[d - 1])
            )

    def place():
        for copy in evict_copies:
            copy.wait_recv()
        new = jnp.zeros(table_ref.shape[2:], F32)
        hits = jnp.zeros((slots, 2 * capacity), F32)
        for i in range(group):
            hit = (slot_id == slots_in[i, :1, : 2 * capacity]) & (slot_lane >= capacity)
            hit = hit.astype(F32)
            hits = hits + hit
            rows = jnp.concatenate([jnp.zeros_like(evict_in[i]), evict_in[i]], axis=0)
            new = new + dot(hit, rows, NN, EXACT)
        written = jnp.sum(hits, axis=1, keepdims=True) > 0.5
        table_out[0, 0] = jnp.where(written, new, table_ref[0, 0])
        for copy in fetch_copies:
            copy.wait_recv()

    stages = (compute, first, second, third, fourth, fifth, sixth, seventh)
    for step in range(n_chunks + len(stages) - 1):
        for s in reversed(range(len(stages))):
            k = step - s
            if 0 <= k < n_chunks:
                stages[s](k)
        if step == 0:
            give()
        if step == n_chunks:
            write_back()
        if step == n_chunks + 2:
            place()
    for copy in pending:
        copy.wait_send()


def fused(
    cache_state,
    table_state,
    batch_idx,
    loss_grad,
    w_first,
    head,
    home,
    fetch_rows,
    fetch_counts,
    evict_rows,
    evict_from,
    evict_counts,
):
    group = lax.axis_size("shard")
    width = w_first.shape[1]
    samples, features = batch_idx.shape[2:]
    cached, state = cache_state.shape[2:]
    slots = table_state.shape[2]
    capacity = fetch_rows.shape[3]
    n_chunks = width // CHUNK
    lists = jnp.concatenate([fetch_rows[0, 0], evict_rows[0, 0], evict_from[0, 0]], axis=1)
    columns = features * cached
    vmem = pl.BlockSpec(memory_space=pltpu.VMEM)
    smem = pl.BlockSpec(memory_space=pltpu.SMEM)
    return pl.pallas_call(
        step_kernel,
        out_shape=(
            jax.ShapeDtypeStruct((w_first.shape[0] // group, width), BF),
            jax.ShapeDtypeStruct(table_state.shape, F32),
            jax.ShapeDtypeStruct((1, 1, group, capacity, state), F32),
        ),
        in_specs=[vmem] * 8 + [smem] * 2,
        out_specs=(vmem, vmem, vmem),
        scratch_shapes=[
            pltpu.VMEM((samples, columns), BF),
            pltpu.VMEM((columns, samples), BF),
            pltpu.VMEM((samples, 128), F32),
            pltpu.VMEM((2, columns, CHUNK), BF),
            pltpu.VMEM((samples, CHUNK), BF),
            pltpu.VMEM((n_chunks, 2, 2, 2, 2, group, PIECE, CHUNK), F32),
            pltpu.VMEM((n_chunks, 2, 2, 2, group, PIECE, CHUNK), F32),
            pltpu.VMEM((n_chunks, 2, 2, group, PIECE, CHUNK), F32),
            pltpu.VMEM((n_chunks, 2, group, PIECE, CHUNK), F32),
            pltpu.VMEM((n_chunks, group, 2, PIECE, CHUNK), F32),
            pltpu.VMEM((n_chunks, group - 1, 2, PIECE, CHUNK), F32),
            pltpu.VMEM((n_chunks, 2, 2, 2, 2, PIECE, CHUNK), F32),
            pltpu.VMEM((group, 8, 128), jnp.int32),
            pltpu.VMEM((group, 8, 128), jnp.int32),
            pltpu.VMEM((group, capacity, state), F32),
            pltpu.VMEM((group, capacity, state), F32),
            pltpu.VMEM((group, capacity, state), F32),
            pltpu.SemaphoreType.DMA((n_chunks * 13,)),
            pltpu.SemaphoreType.DMA((n_chunks * 13,)),
            pltpu.SemaphoreType.DMA((9,)),
            pltpu.SemaphoreType.DMA((9,)),
        ],
        compiler_params=pltpu.CompilerParams(
            collective_id=0, has_side_effects=True, vmem_limit_bytes=48 * 1024 * 1024
        ),
    )(
        cache_state,
        table_state,
        batch_idx,
        loss_grad,
        w_first,
        head[None, :],
        home,
        lists,
        fetch_counts,
        evict_counts,
    )


def solution(mesh):
    placed = (
        P("dp", "shard", None, None),
        P("dp", "shard", None, None),
        P("dp", "shard", None, None),
        P("dp", "shard", None),
        P(),
        P(),
        P("dp", None),
        P("dp", "shard", None, None),
        P("dp", "shard", None),
        P("dp", "shard", None, None),
        P("dp", "shard", None, None),
        P("dp", "shard", None),
    )
    fits = mesh.shape["shard"] == 4 and mesh.shape["dp"] == 8
    return jax.shard_map(
        fused if fits else local,
        mesh=mesh,
        in_specs=placed,
        out_specs=(
            P("shard", None),
            P("dp", "shard", None, None),
            P("dp", "shard", None, None, None),
        ),
        check_vma=False,
    )
```

```python
import functools
import math

import jax
import jax.numpy as jnp
from jax import lax
from jax.experimental import pallas as pl
from jax.experimental.pallas import tpu as pltpu
from jax.sharding import PartitionSpec as P

beta_one = 0.9
beta_two = 0.999
learn_rate = 0.05
epsilon = 1e-08
bias_one = 1.0 - 0.9**10
bias_two = 1.0 - 0.999**10


def adam_rows(state, grads, embed):
    value = state[:, :embed]
    first = state[:, embed : 2 * embed]
    second = state[:, 2 * embed :]
    first = beta_one * first + (1.0 - beta_one) * grads
    second = beta_two * second + (1.0 - beta_two) * grads * grads
    value = value - learn_rate * (first / bias_one) / (jnp.sqrt(second / bias_two) + epsilon)
    return jnp.concatenate([value, first, second], axis=1)


def local(
    cache_state,
    table_state,
    batch_idx,
    loss_grad,
    w_first,
    head,
    home,
    fetch_rows,
    fetch_counts,
    evict_rows,
    evict_from,
    evict_counts,
):
    group = lax.axis_size("shard")
    cache = cache_state[0, 0]
    table = table_state[0, 0]
    batch = batch_idx[0, 0]
    loss = loss_grad[0, 0]
    home_map = home[0]
    wanted = fetch_rows[0, 0]
    gone = evict_rows[0, 0]
    gone_from = evict_from[0, 0]
    width = cache.shape[1]
    embed = width // 3
    table_rows = table.shape[0]
    cache_rows = cache.shape[0]
    capacity = wanted.shape[1]
    mlp_width = w_first.shape[0]
    samples = batch.shape[0]
    within = jnp.arange(capacity, dtype=jnp.int32)[None, :]
    wanted_live = within < fetch_counts[0, 0][:, None]
    gone_live = within < evict_counts[0, 0][:, None]
    place = (
        jnp.take(
            home_map,
            lax.all_to_all(wanted, "shard", split_axis=0, concat_axis=0, tiled=True),
            axis=0,
        )
        % table_rows
    )
    arrived = lax.all_to_all(
        jnp.take(table, place, axis=0), "shard", split_axis=0, concat_axis=0, tiled=True
    )
    flat_batch = batch.reshape(-1)
    looked = jnp.take(cache[:, :embed], flat_batch, axis=0)
    inputs = looked.reshape(samples, mlp_width).astype(jnp.bfloat16)
    pre = jnp.dot(inputs, w_first, preferred_element_type=jnp.float32)
    sigma = jax.nn.sigmoid(pre)
    delta = (loss[:, None] * head[None, :] * sigma * (1.0 + pre * (1.0 - sigma))).astype(
        jnp.bfloat16
    )
    back = lax.dot_general(
        delta, w_first, (((1,), (1,)), ((), ())), preferred_element_type=jnp.float32
    )
    positions = jnp.arange(cache_rows, dtype=jnp.int32)
    onehot = (flat_batch[:, None] == positions[None, :]).astype(jnp.float32)
    grads = lax.dot_general(
        onehot,
        back.reshape(-1, embed),
        (((0,), (0,)), ((), ())),
        precision=lax.Precision.HIGHEST,
        preferred_element_type=jnp.float32,
    )
    updated = adam_rows(cache, grads, embed)
    sent_rows = jnp.take(updated, gone_from.reshape(-1), axis=0).reshape(group, capacity, width)
    sent_slots = jnp.where(gone_live, jnp.take(home_map, gone, axis=0) % table_rows, table_rows)
    got_rows, got_slots = (
        lax.all_to_all(sent_rows, "shard", split_axis=0, concat_axis=0, tiled=True),
        lax.all_to_all(sent_slots, "shard", split_axis=0, concat_axis=0, tiled=True),
    )
    new_table = table.at[got_slots.reshape(-1)].set(got_rows.reshape(-1, width), mode="drop")
    fetched = jnp.where(wanted_live[:, :, None], arrived, jnp.zeros_like(arrived))
    scale = 1.0 / math.sqrt(samples * group * lax.axis_size("dp"))
    partial_rows = lax.psum_scatter(
        lax.dot_general(
            inputs, delta, (((0,), (0,)), ((), ())), preferred_element_type=jnp.float32
        ),
        "shard",
        scatter_dimension=0,
        tiled=True,
    )
    mine = lax.psum(partial_rows, "dp")
    grad_first = (mine * scale).astype(jnp.bfloat16)
    return (grad_first, new_table[None, None], fetched[None, None])


CHUNK = 256
PIECE = 16
BF = jnp.bfloat16
F32 = jnp.float32
EXACT = lax.Precision.HIGHEST


def dot(a, b, dims, precision=None):
    return lax.dot_general(
        a, b, (dims, ((), ())), precision=precision, preferred_element_type=F32
    )


NN = ((1,), (0,))
NT = ((1,), (1,))
TN = ((0,), (0,))


def split_two(a):
    high = a.astype(BF)
    return high, (a - high.astype(F32)).astype(BF)


def step_kernel(
    cache_hbm,
    table_hbm,
    batch_hbm,
    loss_hbm,
    w_hbm,
    head_hbm,
    home_hbm,
    fetch_hbm,
    evict_hbm,
    source_hbm,
    fetch_counts,
    evict_counts,
    grad_out,
    table_out,
    fetched_out,
    hot,
    hot_t,
    loss_col,
    base,
    delta,
    term,
    from_core,
    from_first,
    from_second,
    to_z,
    from_z,
    whole,
    slots_out,
    slots_in,
    rows_out,
    evict_out,
    evict_in,
    sum_send,
    sum_recv,
    row_send,
    row_recv,
    cache_ref,
    table_ref,
    batch_ref,
    loss_ref,
    w_ref,
    head_ref,
    home_ref,
    fetch_ref,
    evict_ref,
    source_ref,
    load_sem,
    by_place,
):
    group = 4
    z = lax.axis_index("shard")
    dp = lax.axis_index("dp")
    core = dp % 2
    x = (dp // 2) % 2
    y = dp // 4
    by_core = {"dp": dp + 1 - 2 * core}
    by_x = {"dp": dp + 2 - 4 * x}
    by_y = {"dp": dp + 4 - 8 * y}
    near = (by_core, by_x, by_y)
    along = [{"shard": (z + d) % group} for d in range(1, group)]

    barrier = pltpu.get_barrier_semaphore()
    for device in near + tuple(along):
        pl.semaphore_signal(
            barrier, inc=1, device_id=device, device_id_type=pl.DeviceIdType.MESH
        )

    loads = {}
    width = w_ref.shape[1]
    n_chunks = width // CHUNK

    def load(name, src, dst):
        loads[name] = pltpu.make_async_copy(src, dst, load_sem.at[len(loads)])
        loads[name].start()

    load("batch", batch_hbm, batch_ref)
    load("cache", cache_hbm, cache_ref)
    load("w0", w_hbm.at[:, pl.ds(0, CHUNK)], w_ref.at[:, pl.ds(0, CHUNK)])
    load("loss", loss_hbm, loss_ref)
    load("head", head_hbm, head_ref)
    load("home", home_hbm, home_ref)
    load("fetch", fetch_hbm, fetch_ref)
    load("evict", evict_hbm, evict_ref)
    load("source", source_hbm, source_ref)
    load("table", table_hbm, table_ref)
    for k in range(1, n_chunks):
        cols = pl.ds(k * CHUNK, CHUNK)
        load(f"w{k}", w_hbm.at[:, cols], w_ref.at[:, cols])

    features, samples = batch_ref.shape[2], batch_ref.shape[3]
    cached = cache_ref.shape[2]
    embed = cache_ref.shape[3] // 3
    slots = table_ref.shape[2]
    capacity = fetched_out.shape[3]
    columns = features * cached

    pending = []

    def send(src, dst, sends, recvs, at, device):
        copy = pltpu.make_async_remote_copy(
            src_ref=src,
            dst_ref=dst,
            send_sem=sends.at[at],
            recv_sem=recvs.at[at],
            device_id=device,
            device_id_type=pl.DeviceIdType.MESH,
        )
        copy.start()
        pending.append(copy)
        return copy

    loads["batch"].wait()
    batch = batch_ref[0, 0].astype(F32).astype(BF)
    at_f = lax.broadcasted_iota(jnp.int32, (features, columns), 0) * cached
    at_c = lax.broadcasted_iota(jnp.int32, (features, columns), 1)
    spread = ((at_c >= at_f) & (at_c < at_f + cached)).astype(F32).astype(BF)
    at_f_t = lax.broadcasted_iota(jnp.int32, (columns, features), 1) * cached
    at_c_t = lax.broadcasted_iota(jnp.int32, (columns, features), 0)
    spread_t = ((at_c_t >= at_f_t) & (at_c_t < at_f_t + cached)).astype(F32).astype(BF)
    own_c = (lax.broadcasted_iota(jnp.int32, (1, columns), 1) % cached).astype(F32)
    one, zero = jnp.float32(1), jnp.float32(0)
    hot[...] = jnp.where(dot(batch, spread, TN) == own_c, one, zero).astype(BF)
    own_c_t = lax.broadcasted_iota(jnp.int32, (cached, samples), 0).astype(F32)
    for f in range(features):
        rows = slice(f * cached, (f + 1) * cached)
        spot = dot(spread_t[rows], batch, NN)
        hot_t[rows, :] = jnp.where(spot == own_c_t, one, zero).astype(BF)
    loads["loss"].wait()
    for t in range(samples // 128):
        piece = loss_ref[0, :, t * 128 : (t + 1) * 128]
        loss_col[t * 128 : (t + 1) * 128, :] = jnp.broadcast_to(piece, (128, 128)).T

    for name in ("home", "fetch", "evict", "source"):
        loads[name].wait()
    home = (home_ref[...] % slots).astype(BF)
    home = jnp.broadcast_to(home.astype(F32), (8, home.shape[1])).astype(BF)
    names = jnp.concatenate([fetch_ref[0, 0], evict_ref[0, 0]], axis=1)
    row_id = lax.broadcasted_iota(jnp.int32, (home.shape[1], 2 * capacity), 0)
    lane = lax.broadcasted_iota(jnp.int32, (8, 2 * capacity), 1)
    for j in range(group):
        hit = (row_id == names[j : j + 1, :]).astype(F32).astype(BF)
        found = dot(home, hit, NN).astype(jnp.int32)
        limit = jnp.where(lane < capacity, fetch_counts[0, 0, j], evict_counts[0, 0, j])
        found = jnp.where(lane % capacity < limit, found, -1)
        slots_out[j] = jnp.full(slots_out.shape[1:], -1, jnp.int32)
        slots_out[j, :, : 2 * capacity] = found
    slots_in[z] = slots_out[z]

    loads["cache"].wait()
    value = cache_ref[0, 0, :, :embed]
    value_bf = value.astype(BF)
    value_t = value.T.astype(BF)
    value_t2 = jnp.concatenate([value_t, value_t], axis=1)

    pl.semaphore_wait(barrier, len(near) + group - 1)
    slot_copies = []
    for d in range(1, group):
        peer = (z + d) % group
        slot_copies.append(
            send(slots_out.at[peer], slots_in.at[z], row_send, row_recv, d - 1, along[d - 1])
        )

    grads = [jnp.zeros((cached, embed), F32)]
    copies = {}
    n_sem = 13

    def forward(k):
        cols = slice(k * CHUNK, (k + 1) * CHUNK)
        loads[f"w{k}"].wait()
        if k == 0:
            loads["head"].wait()
        for f in range(features):
            part = dot(value_bf, w_ref[f * embed : (f + 1) * embed, cols], NN)
            high, low = split_two(part)
            base[0, f * cached : (f + 1) * cached, :] = high
            base[1, f * cached : (f + 1) * cached, :] = low
        head = head_ref[:, cols]
        block = 256

        def rows(t, carry):
            at = pl.ds(pl.multiple_of(t * block, block), block)
            pre = dot(hot[at, :], base[0], NN) + dot(hot[at, :], base[1], NN)
            sigma = 0.5 * jnp.tanh(0.5 * pre) + 0.5
            loss = loss_col[at, :]
            loss = jnp.concatenate([loss] * (CHUNK // 128), axis=1)
            delta[at, :] = (loss * head * sigma * (1.0 + pre * (1.0 - sigma))).astype(BF)
            return carry

        lax.fori_loop(0, samples // block, rows, 0)

    def backward(k):
        cols = slice(k * CHUNK, (k + 1) * CHUNK)
        by_place[...] = dot(hot_t[...], delta[...], NN)
        for f in range(features):
            high, low = split_two(by_place[f * cached : (f + 1) * cached, :])
            both = jnp.concatenate([high, low], axis=0)
            piece = dot(value_t2, both, NN)
            term[k, f % 2, :, :, :, f // 2] = piece.reshape(2, 2, 2, PIECE, CHUNK)
            g = dot(both, w_ref[f * embed : (f + 1) * embed, cols], NT)
            grads[0] = grads[0] + g[:cached] + g[cached:]
        copies[k, 0] = send(
            term.at[k, 1 - core], from_core.at[k], sum_send, sum_recv, k * n_sem, by_core
        )

    def first(k):
        copies[k, 0].wait_recv()
        term[k, core] = term[k, core] + from_core[k]
        copies[k, 1] = send(
            term.at[k, core, 0, 1 - x], from_first.at[k, 0], sum_send, sum_recv, k * n_sem + 1, by_x
        )
        copies[k, 2] = send(
            term.at[k, core, 1, 1 - y], from_first.at[k, 1], sum_send, sum_recv, k * n_sem + 2, by_y
        )

    def second(k):
        copies[k, 1].wait_recv()
        term[k, core, 0, x] = term[k, core, 0, x] + from_first[k, 0]
        copies[k, 3] = send(
            term.at[k, core, 0, x, 1 - y], from_second.at[k, 0], sum_send, sum_recv, k * n_sem + 3, by_y
        )
        copies[k, 2].wait_recv()
        term[k, core, 1, y] = term[k, core, 1, y] + from_first[k, 1]
        copies[k, 4] = send(
            term.at[k, core, 1, y, 1 - x], from_second.at[k, 1], sum_send, sum_recv, k * n_sem + 4, by_x
        )

    def third(k):
        copies[k, 3].wait_recv()
        to_z[k, :, 0] = term[k, core, 0, x, y] + from_second[k, 0]
        copies[k, 4].wait_recv()
        to_z[k, :, 1] = term[k, core, 1, y, x] + from_second[k, 1]
        for d in range(1, group):
            peer = (z + d) % group
            copies[k, 4 + d] = send(
                to_z.at[k, peer], from_z.at[k, d - 1], sum_send, sum_recv, k * n_sem + 4 + d, along[d - 1]
            )

    def fourth(k):
        for d in range(1, group):
            copies[k, 4 + d].wait_recv()
        total = (to_z[k, z] + from_z[k, 0]) + (from_z[k, 1] + from_z[k, 2])
        whole[k, core, 0, x, y] = total[0]
        whole[k, core, 1, y, x] = total[1]
        mine = whole.at[k, core, 0, x, y]
        copies[k, 8] = send(mine, mine, sum_send, sum_recv, k * n_sem + 8, by_y)
        mine = whole.at[k, core, 1, y, x]
        copies[k, 9] = send(mine, mine, sum_send, sum_recv, k * n_sem + 9, by_x)

    def fifth(k):
        copies[k, 8].wait_recv()
        mine = whole.at[k, core, 0, x]
        copies[k, 10] = send(mine, mine, sum_send, sum_recv, k * n_sem + 10, by_x)
        copies[k, 9].wait_recv()
        mine = whole.at[k, core, 1, y]
        copies[k, 11] = send(mine, mine, sum_send, sum_recv, k * n_sem + 11, by_y)

    def sixth(k):
        copies[k, 10].wait_recv()
        copies[k, 11].wait_recv()
        mine = whole.at[k, core]
        copies[k, 12] = send(mine, mine, sum_send, sum_recv, k * n_sem + 12, by_core)

    scale = 1.0 / math.sqrt(samples * 32)

    def seventh(k):
        copies[k, 12].wait_recv()
        got = whole[k].reshape(16 * PIECE, CHUNK)
        grad_out[:, k * CHUNK : (k + 1) * CHUNK] = (got * scale).astype(BF)

    fetch_copies = []
    slot_id = lax.broadcasted_iota(jnp.int32, (slots, 2 * capacity), 0)
    slot_lane = lax.broadcasted_iota(jnp.int32, (slots, 2 * capacity), 1)

    def give():
        loads["table"].wait()
        for copy in slot_copies:
            copy.wait_recv()
        for i in range(group):
            hit = (slot_id == slots_in[i, :1, : 2 * capacity]).astype(F32)
            rows = dot(hit, table_ref[0, 0], TN, EXACT)
            rows_out[i] = rows[:capacity]
        fetched_out[0, 0, z] = rows_out[z]
        for d in range(1, group):
            peer = (z + d) % group
            fetch_copies.append(
                send(rows_out.at[peer], fetched_out.at[0, 0, z], row_send, row_recv, 2 + d, along[d - 1])
            )

    evict_copies = []

    def write_back():
        state = cache_ref[0, 0]
        g = grads[0]
        moment = beta_one * state[:, embed : 2 * embed] + (1.0 - beta_one) * g
        second_moment = beta_two * state[:, 2 * embed :] + (1.0 - beta_two) * g * g
        new = state[:, :embed] - learn_rate * (moment / bias_one) / (
            jnp.sqrt(second_moment / bias_two) + epsilon
        )
        updated = jnp.concatenate([new, moment, second_moment], axis=1)
        position = lax.broadcasted_iota(jnp.int32, (cached, capacity), 0)
        listed = source_ref[0, 0]
        for j in range(group):
            hit = (position == listed[j : j + 1, :]).astype(F32)
            rows = dot(hit, updated, TN, EXACT)
            evict_out[j] = rows
        evict_in[z] = evict_out[z]
        for d in range(1, group):
            peer = (z + d) % group
            evict_copies.append(
                send(evict_out.at[peer], evict_in.at[z], row_send, row_recv, 5 + d, along[d - 1])
            )

    def place():
        for copy in evict_copies:
            copy.wait_recv()
        new = jnp.zeros(table_ref.shape[2:], F32)
        hits = jnp.zeros((slots, 2 * capacity), F32)
        for i in range(group):
            hit = (slot_id == slots_in[i, :1, : 2 * capacity]) & (slot_lane >= capacity)
            hit = hit.astype(F32)
            hits = hits + hit
            rows = jnp.concatenate([jnp.zeros_like(evict_in[i]), evict_in[i]], axis=0)
            new = new + dot(hit, rows, NN, EXACT)
        written = jnp.sum(hits, axis=1, keepdims=True) > 0.5
        table_out[0, 0] = jnp.where(written, new, table_ref[0, 0])
        for copy in fetch_copies:
            copy.wait_recv()

    later = (first, second, third, fourth, fifth, sixth, seventh)
    for step in range(n_chunks + len(later)):
        if step < n_chunks:
            forward(step)
        for s, stage in enumerate(later):
            k = step - 1 - s
            if 0 <= k < n_chunks:
                stage(k)
        if step < n_chunks:
            backward(step)
        if step == 0:
            give()
        if step == n_chunks:
            write_back()
        if step == n_chunks + 2:
            place()
    for copy in pending:
        copy.wait_send()


def fused(
    cache_state,
    table_state,
    batch_idx,
    loss_grad,
    w_first,
    head,
    home,
    fetch_rows,
    fetch_counts,
    evict_rows,
    evict_from,
    evict_counts,
):
    group = lax.axis_size("shard")
    width = w_first.shape[1]
    samples, features = batch_idx.shape[2:]
    cached, state = cache_state.shape[2:]
    slots = table_state.shape[2]
    capacity = fetch_rows.shape[3]
    n_chunks = width // CHUNK
    hbm = pl.BlockSpec(memory_space=pl.ANY)
    columns = features * cached
    vmem = pl.BlockSpec(memory_space=pltpu.VMEM)
    smem = pl.BlockSpec(memory_space=pltpu.SMEM)
    return pl.pallas_call(
        step_kernel,
        out_shape=(
            jax.ShapeDtypeStruct((w_first.shape[0] // group, width), BF),
            jax.ShapeDtypeStruct(table_state.shape, F32),
            jax.ShapeDtypeStruct((1, 1, group, capacity, state), F32),
        ),
        in_specs=[hbm] * 10 + [smem] * 2,
        out_specs=(vmem, vmem, vmem),
        scratch_shapes=[
            pltpu.VMEM((samples, columns), BF),
            pltpu.VMEM((columns, samples), BF),
            pltpu.VMEM((samples, 128), F32),
            pltpu.VMEM((2, columns, CHUNK), BF),
            pltpu.VMEM((samples, CHUNK), BF),
            pltpu.VMEM((n_chunks, 2, 2, 2, 2, group, PIECE, CHUNK), F32),
            pltpu.VMEM((n_chunks, 2, 2, 2, group, PIECE, CHUNK), F32),
            pltpu.VMEM((n_chunks, 2, 2, group, PIECE, CHUNK), F32),
            pltpu.VMEM((n_chunks, 2, group, PIECE, CHUNK), F32),
            pltpu.VMEM((n_chunks, group, 2, PIECE, CHUNK), F32),
            pltpu.VMEM((n_chunks, group - 1, 2, PIECE, CHUNK), F32),
            pltpu.VMEM((n_chunks, 2, 2, 2, 2, PIECE, CHUNK), F32),
            pltpu.VMEM((group, 8, 128), jnp.int32),
            pltpu.VMEM((group, 8, 128), jnp.int32),
            pltpu.VMEM((group, capacity, state), F32),
            pltpu.VMEM((group, capacity, state), F32),
            pltpu.VMEM((group, capacity, state), F32),
            pltpu.SemaphoreType.DMA((n_chunks * 13,)),
            pltpu.SemaphoreType.DMA((n_chunks * 13,)),
            pltpu.SemaphoreType.DMA((9,)),
            pltpu.SemaphoreType.DMA((9,)),
            pltpu.VMEM(cache_state.shape, F32),
            pltpu.VMEM(table_state.shape, F32),
            pltpu.VMEM((1, 1, features, samples), jnp.int32),
            pltpu.VMEM(loss_grad.shape, F32),
            pltpu.VMEM(w_first.shape, BF),
            pltpu.VMEM((1, width), F32),
            pltpu.VMEM(home.shape, jnp.int32),
            pltpu.VMEM(fetch_rows.shape, jnp.int32),
            pltpu.VMEM(evict_rows.shape, jnp.int32),
            pltpu.VMEM(evict_from.shape, jnp.int32),
            pltpu.SemaphoreType.DMA((9 + n_chunks,)),
            pltpu.VMEM((columns, CHUNK), F32),
        ],
        compiler_params=pltpu.CompilerParams(
            collective_id=0, has_side_effects=True, vmem_limit_bytes=56 * 1024 * 1024
        ),
    )(
        cache_state,
        table_state,
        jnp.swapaxes(batch_idx, 2, 3),
        loss_grad,
        w_first,
        head[None, :],
        home,
        fetch_rows,
        evict_rows,
        evict_from,
        fetch_counts,
        evict_counts,
    )


def solution(mesh):
    placed = (
        P("dp", "shard", None, None),
        P("dp", "shard", None, None),
        P("dp", "shard", None, None),
        P("dp", "shard", None),
        P(),
        P(),
        P("dp", None),
        P("dp", "shard", None, None),
        P("dp", "shard", None),
        P("dp", "shard", None, None),
        P("dp", "shard", None, None),
        P("dp", "shard", None),
    )
    fits = mesh.shape["shard"] == 4 and mesh.shape["dp"] == 8
    return jax.shard_map(
        fused if fits else local,
        mesh=mesh,
        in_specs=placed,
        out_specs=(
            P("shard", None),
            P("dp", "shard", None, None),
            P("dp", "shard", None, None, None),
        ),
        check_vma=False,
    )
```

```python
import functools
import math

import jax
import jax.numpy as jnp
from jax import lax
from jax.experimental import pallas as pl
from jax.experimental.pallas import tpu as pltpu
from jax.sharding import PartitionSpec as P

beta_one = 0.9
beta_two = 0.999
learn_rate = 0.05
epsilon = 1e-08
bias_one = 1.0 - 0.9**10
bias_two = 1.0 - 0.999**10


def adam_rows(state, grads, embed):
    value = state[:, :embed]
    first = state[:, embed : 2 * embed]
    second = state[:, 2 * embed :]
    first = beta_one * first + (1.0 - beta_one) * grads
    second = beta_two * second + (1.0 - beta_two) * grads * grads
    value = value - learn_rate * (first / bias_one) / (jnp.sqrt(second / bias_two) + epsilon)
    return jnp.concatenate([value, first, second], axis=1)


def local(
    cache_state,
    table_state,
    batch_idx,
    loss_grad,
    w_first,
    head,
    home,
    fetch_rows,
    fetch_counts,
    evict_rows,
    evict_from,
    evict_counts,
):
    group = lax.axis_size("shard")
    cache = cache_state[0, 0]
    table = table_state[0, 0]
    batch = batch_idx[0, 0]
    loss = loss_grad[0, 0]
    home_map = home[0]
    wanted = fetch_rows[0, 0]
    gone = evict_rows[0, 0]
    gone_from = evict_from[0, 0]
    width = cache.shape[1]
    embed = width // 3
    table_rows = table.shape[0]
    cache_rows = cache.shape[0]
    capacity = wanted.shape[1]
    mlp_width = w_first.shape[0]
    samples = batch.shape[0]
    within = jnp.arange(capacity, dtype=jnp.int32)[None, :]
    wanted_live = within < fetch_counts[0, 0][:, None]
    gone_live = within < evict_counts[0, 0][:, None]
    place = (
        jnp.take(
            home_map,
            lax.all_to_all(wanted, "shard", split_axis=0, concat_axis=0, tiled=True),
            axis=0,
        )
        % table_rows
    )
    arrived = lax.all_to_all(
        jnp.take(table, place, axis=0), "shard", split_axis=0, concat_axis=0, tiled=True
    )
    flat_batch = batch.reshape(-1)
    looked = jnp.take(cache[:, :embed], flat_batch, axis=0)
    inputs = looked.reshape(samples, mlp_width).astype(jnp.bfloat16)
    pre = jnp.dot(inputs, w_first, preferred_element_type=jnp.float32)
    sigma = jax.nn.sigmoid(pre)
    delta = (loss[:, None] * head[None, :] * sigma * (1.0 + pre * (1.0 - sigma))).astype(
        jnp.bfloat16
    )
    back = lax.dot_general(
        delta, w_first, (((1,), (1,)), ((), ())), preferred_element_type=jnp.float32
    )
    positions = jnp.arange(cache_rows, dtype=jnp.int32)
    onehot = (flat_batch[:, None] == positions[None, :]).astype(jnp.float32)
    grads = lax.dot_general(
        onehot,
        back.reshape(-1, embed),
        (((0,), (0,)), ((), ())),
        precision=lax.Precision.HIGHEST,
        preferred_element_type=jnp.float32,
    )
    updated = adam_rows(cache, grads, embed)
    sent_rows = jnp.take(updated, gone_from.reshape(-1), axis=0).reshape(group, capacity, width)
    sent_slots = jnp.where(gone_live, jnp.take(home_map, gone, axis=0) % table_rows, table_rows)
    got_rows, got_slots = (
        lax.all_to_all(sent_rows, "shard", split_axis=0, concat_axis=0, tiled=True),
        lax.all_to_all(sent_slots, "shard", split_axis=0, concat_axis=0, tiled=True),
    )
    new_table = table.at[got_slots.reshape(-1)].set(got_rows.reshape(-1, width), mode="drop")
    fetched = jnp.where(wanted_live[:, :, None], arrived, jnp.zeros_like(arrived))
    scale = 1.0 / math.sqrt(samples * group * lax.axis_size("dp"))
    partial_rows = lax.psum_scatter(
        lax.dot_general(
            inputs, delta, (((0,), (0,)), ((), ())), preferred_element_type=jnp.float32
        ),
        "shard",
        scatter_dimension=0,
        tiled=True,
    )
    mine = lax.psum(partial_rows, "dp")
    grad_first = (mine * scale).astype(jnp.bfloat16)
    return (grad_first, new_table[None, None], fetched[None, None])


CHUNK = 256
PIECE = 16
BF = jnp.bfloat16
F32 = jnp.float32
EXACT = lax.Precision.HIGHEST


def dot(a, b, dims, precision=None):
    return lax.dot_general(
        a, b, (dims, ((), ())), precision=precision, preferred_element_type=F32
    )


NN = ((1,), (0,))
NT = ((1,), (1,))
TN = ((0,), (0,))


def split_two(a):
    high = a.astype(BF)
    return high, (a - high.astype(F32)).astype(BF)


def step_kernel(
    cache_hbm,
    table_hbm,
    batch_hbm,
    loss_hbm,
    w_hbm,
    head_hbm,
    home_hbm,
    fetch_hbm,
    evict_hbm,
    source_hbm,
    fetch_counts,
    evict_counts,
    grad_out,
    table_out,
    fetched_out,
    hot,
    hot_t,
    loss_col,
    base,
    delta,
    term,
    from_core,
    from_first,
    from_second,
    to_z,
    from_z,
    whole,
    slots_out,
    slots_in,
    rows_out,
    evict_out,
    evict_in,
    sum_send,
    sum_recv,
    row_send,
    row_recv,
    cache_ref,
    table_ref,
    batch_ref,
    loss_ref,
    w_ref,
    head_ref,
    home_ref,
    fetch_ref,
    evict_ref,
    source_ref,
    load_sem,
    by_place,
):
    group = 4
    z = lax.axis_index("shard")
    dp = lax.axis_index("dp")
    core = dp % 2
    x = (dp // 2) % 2
    y = dp // 4
    by_core = {"dp": dp + 1 - 2 * core}
    by_x = {"dp": dp + 2 - 4 * x}
    by_y = {"dp": dp + 4 - 8 * y}
    by_both = {"dp": dp + 6 - 4 * x - 8 * y}
    near = (by_core, by_x, by_y, by_both)
    along = [{"shard": (z + d) % group} for d in range(1, group)]

    barrier = pltpu.get_barrier_semaphore()
    for device in near + tuple(along):
        pl.semaphore_signal(
            barrier, inc=1, device_id=device, device_id_type=pl.DeviceIdType.MESH
        )

    loads = {}
    width = w_ref.shape[1]
    n_chunks = width // CHUNK

    def load(name, src, dst):
        loads[name] = pltpu.make_async_copy(src, dst, load_sem.at[len(loads)])
        loads[name].start()

    load("batch", batch_hbm, batch_ref)
    load("cache", cache_hbm, cache_ref)
    load("w0", w_hbm.at[:, pl.ds(0, CHUNK)], w_ref.at[:, pl.ds(0, CHUNK)])
    load("loss", loss_hbm, loss_ref)
    load("head", head_hbm, head_ref)
    load("home", home_hbm, home_ref)
    load("fetch", fetch_hbm, fetch_ref)
    load("evict", evict_hbm, evict_ref)
    load("source", source_hbm, source_ref)
    load("table", table_hbm, table_ref)
    for k in range(1, n_chunks):
        cols = pl.ds(k * CHUNK, CHUNK)
        load(f"w{k}", w_hbm.at[:, cols], w_ref.at[:, cols])

    features, samples = batch_ref.shape[2], batch_ref.shape[3]
    cached = cache_ref.shape[2]
    embed = cache_ref.shape[3] // 3
    slots = table_ref.shape[2]
    capacity = fetched_out.shape[3]
    columns = features * cached

    pending = []

    def send(src, dst, sends, recvs, at, device):
        copy = pltpu.make_async_remote_copy(
            src_ref=src,
            dst_ref=dst,
            send_sem=sends.at[at],
            recv_sem=recvs.at[at],
            device_id=device,
            device_id_type=pl.DeviceIdType.MESH,
        )
        copy.start()
        pending.append(copy)
        return copy

    loads["batch"].wait()
    batch = batch_ref[0, 0].astype(F32).astype(BF)
    at_f = lax.broadcasted_iota(jnp.int32, (features, columns), 0) * cached
    at_c = lax.broadcasted_iota(jnp.int32, (features, columns), 1)
    spread = ((at_c >= at_f) & (at_c < at_f + cached)).astype(F32).astype(BF)
    at_f_t = lax.broadcasted_iota(jnp.int32, (columns, features), 1) * cached
    at_c_t = lax.broadcasted_iota(jnp.int32, (columns, features), 0)
    spread_t = ((at_c_t >= at_f_t) & (at_c_t < at_f_t + cached)).astype(F32).astype(BF)
    own_c = (lax.broadcasted_iota(jnp.int32, (1, columns), 1) % cached).astype(F32)
    one, zero = jnp.float32(1), jnp.float32(0)
    hot[...] = jnp.where(dot(batch, spread, TN) == own_c, one, zero).astype(BF)
    own_c_t = lax.broadcasted_iota(jnp.int32, (cached, samples), 0).astype(F32)
    for f in range(features):
        rows = slice(f * cached, (f + 1) * cached)
        spot = dot(spread_t[rows], batch, NN)
        hot_t[rows, :] = jnp.where(spot == own_c_t, one, zero).astype(BF)
    loads["loss"].wait()
    for t in range(samples // 128):
        piece = loss_ref[0, :, t * 128 : (t + 1) * 128]
        loss_col[t * 128 : (t + 1) * 128, :] = jnp.broadcast_to(piece, (128, 128)).T

    for name in ("home", "fetch", "evict", "source"):
        loads[name].wait()
    home = (home_ref[...] % slots).astype(BF)
    home = jnp.broadcast_to(home.astype(F32), (8, home.shape[1])).astype(BF)
    names = jnp.concatenate([fetch_ref[0, 0], evict_ref[0, 0]], axis=1)
    row_id = lax.broadcasted_iota(jnp.int32, (home.shape[1], 2 * capacity), 0)
    lane = lax.broadcasted_iota(jnp.int32, (8, 2 * capacity), 1)
    for j in range(group):
        hit = (row_id == names[j : j + 1, :]).astype(F32).astype(BF)
        found = dot(home, hit, NN).astype(jnp.int32)
        limit = jnp.where(lane < capacity, fetch_counts[0, 0, j], evict_counts[0, 0, j])
        found = jnp.where(lane % capacity < limit, found, -1)
        slots_out[j] = jnp.full(slots_out.shape[1:], -1, jnp.int32)
        slots_out[j, :, : 2 * capacity] = found
    slots_in[z] = slots_out[z]

    loads["cache"].wait()
    value = cache_ref[0, 0, :, :embed]
    value_bf = value.astype(BF)
    value_t = value.T.astype(BF)
    value_t2 = jnp.concatenate([value_t, value_t], axis=1)

    pl.semaphore_wait(barrier, len(near) + group - 1)
    slot_copies = []
    for d in range(1, group):
        peer = (z + d) % group
        slot_copies.append(
            send(slots_out.at[peer], slots_in.at[z], row_send, row_recv, d - 1, along[d - 1])
        )

    grads = [jnp.zeros((cached, embed), F32)]
    copies = {}
    n_sem = 15

    def forward(k):
        cols = slice(k * CHUNK, (k + 1) * CHUNK)
        loads[f"w{k}"].wait()
        if k == 0:
            loads["head"].wait()
        for f in range(features):
            part = dot(value_bf, w_ref[f * embed : (f + 1) * embed, cols], NN)
            high, low = split_two(part)
            base[0, f * cached : (f + 1) * cached, :] = high
            base[1, f * cached : (f + 1) * cached, :] = low
        head = head_ref[:, cols]
        block = 256

        def rows(t, carry):
            at = pl.ds(pl.multiple_of(t * block, block), block)
            pre = dot(hot[at, :], base[0], NN) + dot(hot[at, :], base[1], NN)
            sigma = 0.5 * jnp.tanh(0.5 * pre) + 0.5
            loss = loss_col[at, :]
            loss = jnp.concatenate([loss] * (CHUNK // 128), axis=1)
            delta[at, :] = (loss * head * sigma * (1.0 + pre * (1.0 - sigma))).astype(BF)
            return carry

        lax.fori_loop(0, samples // block, rows, 0)

    def backward(k):
        cols = slice(k * CHUNK, (k + 1) * CHUNK)
        by_place[...] = dot(hot_t[...], delta[...], NN)
        for f in range(features):
            high, low = split_two(by_place[f * cached : (f + 1) * cached, :])
            both = jnp.concatenate([high, low], axis=0)
            piece = dot(value_t2, both, NN)
            term[k, f % 2, :, :, :, f // 2] = piece.reshape(2, 2, 2, PIECE, CHUNK)
            g = dot(both, w_ref[f * embed : (f + 1) * embed, cols], NT)
            grads[0] = grads[0] + g[:cached] + g[cached:]
        copies[k, 0] = send(
            term.at[k, 1 - core], from_core.at[k], sum_send, sum_recv, k * n_sem, by_core
        )

    def first(k):
        copies[k, 0].wait_recv()
        term[k, core] = term[k, core] + from_core[k]
        copies[k, 1] = send(
            term.at[k, core, 0, 1 - x], from_first.at[k, 0], sum_send, sum_recv, k * n_sem + 1, by_x
        )
        copies[k, 2] = send(
            term.at[k, core, 1, 1 - y], from_first.at[k, 1], sum_send, sum_recv, k * n_sem + 2, by_y
        )

    def second(k):
        copies[k, 1].wait_recv()
        term[k, core, 0, x] = term[k, core, 0, x] + from_first[k, 0]
        copies[k, 3] = send(
            term.at[k, core, 0, x, 1 - y], from_second.at[k, 0], sum_send, sum_recv, k * n_sem + 3, by_y
        )
        copies[k, 2].wait_recv()
        term[k, core, 1, y] = term[k, core, 1, y] + from_first[k, 1]
        copies[k, 4] = send(
            term.at[k, core, 1, y, 1 - x], from_second.at[k, 1], sum_send, sum_recv, k * n_sem + 4, by_x
        )

    def third(k):
        copies[k, 3].wait_recv()
        to_z[k, :, 0] = term[k, core, 0, x, y] + from_second[k, 0]
        copies[k, 4].wait_recv()
        to_z[k, :, 1] = term[k, core, 1, y, x] + from_second[k, 1]
        for d in range(1, group):
            peer = (z + d) % group
            copies[k, 4 + d] = send(
                to_z.at[k, peer], from_z.at[k, d - 1], sum_send, sum_recv, k * n_sem + 4 + d, along[d - 1]
            )

    def fourth(k):
        for d in range(1, group):
            copies[k, 4 + d].wait_recv()
        total = (to_z[k, z] + from_z[k, 0]) + (from_z[k, 1] + from_z[k, 2])
        whole[k, core, 0, x, y] = total[0]
        whole[k, core, 1, y, x] = total[1]
        at = 8
        for mine in (whole.at[k, core, 0, x, y], whole.at[k, core, 1, y, x]):
            for device in (by_both, by_x, by_y):
                copies[k, at] = send(
                    mine, mine, sum_send, sum_recv, k * n_sem + at, device
                )
                at += 1

    def fifth(k):
        for at in range(8, 14):
            copies[k, at].wait_recv()
        mine = whole.at[k, core]
        copies[k, 14] = send(mine, mine, sum_send, sum_recv, k * n_sem + 14, by_core)

    scale = 1.0 / math.sqrt(samples * 32)

    def sixth(k):
        copies[k, 14].wait_recv()
        got = whole[k].reshape(16 * PIECE, CHUNK)
        grad_out[:, k * CHUNK : (k + 1) * CHUNK] = (got * scale).astype(BF)

    fetch_copies = []
    slot_id = lax.broadcasted_iota(jnp.int32, (slots, 2 * capacity), 0)
    slot_lane = lax.broadcasted_iota(jnp.int32, (slots, 2 * capacity), 1)

    def give():
        loads["table"].wait()
        for copy in slot_copies:
            copy.wait_recv()
        for i in range(group):
            hit = (slot_id == slots_in[i, :1, : 2 * capacity]).astype(F32)
            rows = dot(hit, table_ref[0, 0], TN, EXACT)
            rows_out[i] = rows[:capacity]
        fetched_out[0, 0, z] = rows_out[z]
        for d in range(1, group):
            peer = (z + d) % group
            fetch_copies.append(
                send(rows_out.at[peer], fetched_out.at[0, 0, z], row_send, row_recv, 2 + d, along[d - 1])
            )

    evict_copies = []

    def write_back():
        state = cache_ref[0, 0]
        g = grads[0]
        moment = beta_one * state[:, embed : 2 * embed] + (1.0 - beta_one) * g
        second_moment = beta_two * state[:, 2 * embed :] + (1.0 - beta_two) * g * g
        new = state[:, :embed] - learn_rate * (moment / bias_one) / (
            jnp.sqrt(second_moment / bias_two) + epsilon
        )
        updated = jnp.concatenate([new, moment, second_moment], axis=1)
        position = lax.broadcasted_iota(jnp.int32, (cached, capacity), 0)
        listed = source_ref[0, 0]
        for j in range(group):
            hit = (position == listed[j : j + 1, :]).astype(F32)
            rows = dot(hit, updated, TN, EXACT)
            evict_out[j] = rows
        evict_in[z] = evict_out[z]
        for d in range(1, group):
            peer = (z + d) % group
            evict_copies.append(
                send(evict_out.at[peer], evict_in.at[z], row_send, row_recv, 5 + d, along[d - 1])
            )

    def place():
        for copy in evict_copies:
            copy.wait_recv()
        new = jnp.zeros(table_ref.shape[2:], F32)
        hits = jnp.zeros((slots, 2 * capacity), F32)
        for i in range(group):
            hit = (slot_id == slots_in[i, :1, : 2 * capacity]) & (slot_lane >= capacity)
            hit = hit.astype(F32)
            hits = hits + hit
            rows = jnp.concatenate([jnp.zeros_like(evict_in[i]), evict_in[i]], axis=0)
            new = new + dot(hit, rows, NN, EXACT)
        written = jnp.sum(hits, axis=1, keepdims=True) > 0.5
        table_out[0, 0] = jnp.where(written, new, table_ref[0, 0])
        for copy in fetch_copies:
            copy.wait_recv()

    later = (first, second, third, fourth, fifth, sixth)
    for step in range(n_chunks + len(later)):
        if step < n_chunks:
            forward(step)
        for s, stage in enumerate(later):
            k = step - 1 - s
            if 0 <= k < n_chunks:
                stage(k)
        if step < n_chunks:
            backward(step)
        if step == n_chunks:
            write_back()
        if step == n_chunks + 1:
            give()
        if step == n_chunks + 3:
            place()
    for copy in pending:
        copy.wait_send()


def fused(
    cache_state,
    table_state,
    batch_idx,
    loss_grad,
    w_first,
    head,
    home,
    fetch_rows,
    fetch_counts,
    evict_rows,
    evict_from,
    evict_counts,
):
    group = lax.axis_size("shard")
    width = w_first.shape[1]
    samples, features = batch_idx.shape[2:]
    cached, state = cache_state.shape[2:]
    slots = table_state.shape[2]
    capacity = fetch_rows.shape[3]
    n_chunks = width // CHUNK
    hbm = pl.BlockSpec(memory_space=pl.ANY)
    columns = features * cached
    vmem = pl.BlockSpec(memory_space=pltpu.VMEM)
    smem = pl.BlockSpec(memory_space=pltpu.SMEM)
    return pl.pallas_call(
        step_kernel,
        out_shape=(
            jax.ShapeDtypeStruct((w_first.shape[0] // group, width), BF),
            jax.ShapeDtypeStruct(table_state.shape, F32),
            jax.ShapeDtypeStruct((1, 1, group, capacity, state), F32),
        ),
        in_specs=[hbm] * 10 + [smem] * 2,
        out_specs=(vmem, vmem, vmem),
        scratch_shapes=[
            pltpu.VMEM((samples, columns), BF),
            pltpu.VMEM((columns, samples), BF),
            pltpu.VMEM((samples, 128), F32),
            pltpu.VMEM((2, columns, CHUNK), BF),
            pltpu.VMEM((samples, CHUNK), BF),
            pltpu.VMEM((n_chunks, 2, 2, 2, 2, group, PIECE, CHUNK), F32),
            pltpu.VMEM((n_chunks, 2, 2, 2, group, PIECE, CHUNK), F32),
            pltpu.VMEM((n_chunks, 2, 2, group, PIECE, CHUNK), F32),
            pltpu.VMEM((n_chunks, 2, group, PIECE, CHUNK), F32),
            pltpu.VMEM((n_chunks, group, 2, PIECE, CHUNK), F32),
            pltpu.VMEM((n_chunks, group - 1, 2, PIECE, CHUNK), F32),
            pltpu.VMEM((n_chunks, 2, 2, 2, 2, PIECE, CHUNK), F32),
            pltpu.VMEM((group, 8, 128), jnp.int32),
            pltpu.VMEM((group, 8, 128), jnp.int32),
            pltpu.VMEM((group, capacity, state), F32),
            pltpu.VMEM((group, capacity, state), F32),
            pltpu.VMEM((group, capacity, state), F32),
            pltpu.SemaphoreType.DMA((n_chunks * 15,)),
            pltpu.SemaphoreType.DMA((n_chunks * 15,)),
            pltpu.SemaphoreType.DMA((9,)),
            pltpu.SemaphoreType.DMA((9,)),
            pltpu.VMEM(cache_state.shape, F32),
            pltpu.VMEM(table_state.shape, F32),
            pltpu.VMEM((1, 1, features, samples), jnp.int32),
            pltpu.VMEM(loss_grad.shape, F32),
            pltpu.VMEM(w_first.shape, BF),
            pltpu.VMEM((1, width), F32),
            pltpu.VMEM(home.shape, jnp.int32),
            pltpu.VMEM(fetch_rows.shape, jnp.int32),
            pltpu.VMEM(evict_rows.shape, jnp.int32),
            pltpu.VMEM(evict_from.shape, jnp.int32),
            pltpu.SemaphoreType.DMA((9 + n_chunks,)),
            pltpu.VMEM((columns, CHUNK), F32),
        ],
        compiler_params=pltpu.CompilerParams(
            collective_id=0, has_side_effects=True, vmem_limit_bytes=56 * 1024 * 1024
        ),
    )(
        cache_state,
        table_state,
        jnp.swapaxes(batch_idx, 2, 3),
        loss_grad,
        w_first,
        head[None, :],
        home,
        fetch_rows,
        evict_rows,
        evict_from,
        fetch_counts,
        evict_counts,
    )


def solution(mesh):
    placed = (
        P("dp", "shard", None, None),
        P("dp", "shard", None, None),
        P("dp", "shard", None, None),
        P("dp", "shard", None),
        P(),
        P(),
        P("dp", None),
        P("dp", "shard", None, None),
        P("dp", "shard", None),
        P("dp", "shard", None, None),
        P("dp", "shard", None, None),
        P("dp", "shard", None),
    )
    fits = mesh.shape["shard"] == 4 and mesh.shape["dp"] == 8
    return jax.shard_map(
        fused if fits else local,
        mesh=mesh,
        in_specs=placed,
        out_specs=(
            P("shard", None),
            P("dp", "shard", None, None),
            P("dp", "shard", None, None, None),
        ),
        check_vma=False,
    )
```
